32 devices in a mesh: wide: 8 (over z, y), narrow: 4 (over x, core).
Axes of the slice: x: 2, y: 2, z: 4, core: 2. Of those that a mesh axis runs over, the one named last changes fastest.
Arguments:
- patches: bfloat16 [2048, 1280], P('wide', 'narrow'), may hold values from -6 to 6
- window_ids: int32 [8, 64], P('wide'), may hold values from 0 to 31, never falling along the last dimension, each value on 1 to 16 neighbouring positions
- vit_gain: float32 [1280], replicated, may hold values from 0.25 to 1.75
- vit_qkv: bfloat16 [3, 1280, 1280], P(None, None, 'narrow'), may hold values from -0.15625 to 0.15625
- vit_qkv_bias: float32 [3, 1280], P(None, 'narrow'), may hold values from -3 to 3
- vit_proj: bfloat16 [1280, 1280], P('narrow'), may hold values from -0.15625 to 0.15625
- vit_proj_bias: float32 [1280], replicated, may hold values from -3 to 3
- merge_gain: float32 [1280], replicated, may hold values from 0.25 to 1.75
- merge_up: bfloat16 [5120, 5120], P(None, 'narrow'), may hold values from -0.078125 to 0.078125
- merge_up_bias: float32 [5120], P('narrow'), may hold values from -3 to 3
- merge_down: bfloat16 [5120, 8192], P('narrow'), may hold values from -0.078125 to 0.078125
- merge_down_bias: float32 [8192], replicated, may hold values from -3 to 3
- input_gain: float32 [8192], replicated, may hold values from 0.25 to 1.75
- kv_weight: bfloat16 [2, 8192, 1024], P(None, None, 'narrow'), may hold values from -0.0625 to 0.0625
- kv_bias: float32 [2, 1024], P(None, 'narrow'), may hold values from -3 to 3
- key_positions: int32 [3, 512], P(None, 'wide'), may hold values from 0 to 8191
- queries: bfloat16 [32, 64, 8192], P('wide', None, 'narrow'), may hold values from -70 to 70
- question_kv: bfloat16 [2, 32, 64, 1024], P(None, 'wide', None, 'narrow'), may hold values from -8 to 8
- question_start: int32 [32], P('wide'), may hold values from 8192 to 16383
- question_length: int32 [32], P('wide'), may hold values from 1 to 64, 1280 in all
Outputs:
- attended: bfloat16 [32, 64, 8192], P('wide', None, 'narrow')
- kv_cache: bfloat16 [2, 512, 1024], P(None, 'wide', 'narrow')
The draws below stay inside these ranges and needn't reach their ends.
Inputs may be any that keep to these rules, and one draw needn't show every extreme that they name: `window_ids`: each row holds the window numbers of one index of wide's merged tokens in order; numbers never fall along a row, a window holds 1 to 16 merged tokens, and some window holds exactly 16. `question_length`: some question has all 64 tokens live.
All inputs are finite; a program needn't handle non-finite values. No bound on the sum of `question_length` on one device may be relied on, other than what follows from the above.
Results may differ from the reference program's by a relative error of at most 0.024.
Values may be sent and summed in bfloat16 or wider, within the bound.
A program may use at most 320 MiB of HBM per device.

```python
import math
import jax
import jax.numpy as jnp
import numpy as np
from jax import lax

D = 8192
HEADS = 64
KV_HEADS = 8
HD = 128
VD = 1280
VHEADS = 16
MH = 5120
VHD = 80
QLEN = 64
WIN_MERGED = 16
MERGED_DEV = 64
MERGED = 512
PATCHES = 2048
QUESTIONS = 32
WIDE_ROWS = 8
N_WIDE = 8


def draw_queries(key, part):
    key = jax.random.fold_in(key, 7)
    first = jax.random.fold_in(key, 0)
    shape = (QUESTIONS, QLEN, HEADS * HD)
    return jnp.clip(jax.random.normal(first, shape, jnp.float32), -6.0, 6.0).astype(jnp.bfloat16)


def touch_ends(entries, key, least, high):
    index_at = [jax.random.randint(jax.random.fold_in(key, axis), (), 0, length) for axis, length in enumerate(entries.shape)]
    widest = entries.shape.index(max(entries.shape))
    beside = index_at[:widest] + [(index_at[widest] + 1) % entries.shape[widest]] + index_at[widest + 1:]
    return entries.at[tuple(index_at)].set(least).at[tuple(beside)].set(high)


def steps_of(stream_key, shape, cuts, low, high):
    level, own = 1.0, jax.random.fold_in(stream_key, 6)
    for axis_at, blocks in cuts:
        steps = jnp.exp(jax.random.uniform(jax.random.fold_in(own, axis_at), (blocks,), jnp.float32, low / len(cuts), high / len(cuts)))
        level = level * jnp.repeat(steps, shape[axis_at] // blocks).reshape([-1 if axis == axis_at else 1 for axis in range(len(shape))])
    return level


def length_profile(count, total, most, slope):
    loads = [(1 << 20) // math.isqrt(grade ** slope) + 1 for grade in range(2, count + 1)]
    rest, holding = total - most - (count - 1), [1] * (count - 1)
    while rest > 0:
        free = [i for i in range(count - 1) if holding[i] < most]
        whole, budget = sum([loads[i] for i in free]), rest
        for i in free:
            more = min(most - holding[i], max(1, budget * loads[i] // whole), rest)
            holding[i] = holding[i] + more
            rest = rest - more
    return np.array([most] + holding)


def ragged(own_key, number_of, total, bound, skew):
    if number_of == 2:
        one = jax.random.randint(own_key, (), max(1, total - bound), min(bound, total - 1) + 1)
        return jnp.stack([one, total - one])
    tallies = jnp.asarray(length_profile(number_of, total, bound, skew), jnp.int32)
    twos = (number_of - 1) // 2
    source_of, sink = tallies[1:1 + 2 * twos:2], tallies[2:2 + 2 * twos:2]
    margin = jnp.minimum(source_of - 1, bound - sink)
    moved = jax.random.randint(jax.random.fold_in(own_key, 1), (twos,), 0, 1 << 20) % (margin + 1)
    tallies = tallies.at[1:1 + 2 * twos:2].set(source_of - moved).at[2:2 + 2 * twos:2].set(sink + moved)
    return tallies[jax.random.permutation(jax.random.fold_in(own_key, 2), number_of)]


def gaussian(stream_key, extent, spread, bound, cuts=(), kind=jnp.bfloat16):
    level = steps_of(stream_key, extent, cuts, -0.22, 0.18) if cuts else 1.0
    result = jax.random.normal(stream_key, extent, jnp.float32) * spread * level
    return jnp.minimum(jnp.maximum(result, -bound), bound).astype(kind)


def setup_inputs(seed: int = 0) -> dict:
    splits = jax.random.split(jax.random.key(seed), 21)
    patches = gaussian(splits[0], (PATCHES, VD), 1.0, 6.0, ((0, 8), (1, 4)))
    window_ids = jax.vmap(lambda own: jnp.searchsorted(jnp.cumsum(ragged(own, MERGED_DEV // 2, MERGED_DEV, WIN_MERGED, 1)), jnp.arange(MERGED_DEV), side="right"))(jax.random.split(splits[1], WIDE_ROWS)).reshape((WIDE_ROWS, MERGED_DEV)).astype(jnp.int32)
    vit_gain = jnp.clip(1.0 + 0.15 * jax.random.normal(splits[2], (VD,), jnp.float32), 0.25, 1.75)
    vit_qkv = gaussian(splits[3], (3, VD, VD), VD ** -0.5, 0.15625, ((2, 4),))
    vit_qkv_bias = gaussian(splits[4], (3, VD), 0.5, 3.0, ((1, 4),), jnp.float32)
    vit_proj = gaussian(splits[5], (VD, VD), VD ** -0.5, 0.15625, ((0, 4),))
    vit_proj_bias = gaussian(splits[6], (VD,), 0.5, 3.0, (), jnp.float32)
    merge_gain = jnp.clip(1.0 + 0.15 * jax.random.normal(splits[7], (VD,), jnp.float32), 0.25, 1.75)
    merge_up = gaussian(splits[8], (4 * VD, MH), (4 * VD) ** -0.5, 0.078125, ((1, 4),))
    merge_up_bias = gaussian(splits[9], (MH,), 0.5, 3.0, ((0, 4),), jnp.float32)
    merge_down = gaussian(splits[10], (MH, D), MH ** -0.5, 0.078125, ((0, 4),))
    merge_down_bias = gaussian(splits[11], (D,), 0.5, 3.0, (), jnp.float32)
    input_gain = jnp.clip(1.0 + 0.15 * jax.random.normal(splits[12], (D,), jnp.float32), 0.25, 1.75)
    kv_weight = gaussian(splits[13], (2, D, KV_HEADS * HD), D ** -0.5, 0.0625, ((2, 4),))
    kv_bias = gaussian(splits[14], (2, KV_HEADS * HD), 0.5, 3.0, ((1, 4),), jnp.float32)
    key_positions = touch_ends(jax.random.randint(splits[15], (3, MERGED), 0, 8192), jax.random.fold_in(splits[15], 1), 0, 8191).astype(jnp.int32)
    queries = draw_queries(jax.random.fold_in(splits[20], 71), 0)
    question_kv = gaussian(splits[17], (2, QUESTIONS, QLEN, KV_HEADS * HD), 1.5, 8.0, ((1, 8), (3, 4)))
    question_start = touch_ends(jax.random.randint(splits[18], (QUESTIONS,), 8192, 16384), jax.random.fold_in(splits[18], 1), 8192, 16383).astype(jnp.int32)
    question_length = ragged(splits[19], QUESTIONS, QUESTIONS * (5 * QLEN // 8), QLEN, 2).astype(jnp.int32)
    return {"patches": patches, "window_ids": window_ids, "vit_gain": vit_gain, "vit_qkv": vit_qkv, "vit_qkv_bias": vit_qkv_bias, "vit_proj": vit_proj, "vit_proj_bias": vit_proj_bias, "merge_gain": merge_gain, "merge_up": merge_up, "merge_up_bias": merge_up_bias, "merge_down": merge_down, "merge_down_bias": merge_down_bias, "input_gain": input_gain, "kv_weight": kv_weight, "kv_bias": kv_bias, "key_positions": key_positions, "queries": queries, "question_kv": question_kv, "question_start": question_start, "question_length": question_length}


def rms_scale(values_in, gain):
    return values_in * lax.rsqrt(lax.optimization_barrier(jnp.mean(values_in * values_in, axis=-1, keepdims=True)) + 1e-06) * gain.astype(jnp.float32)

def rotate_pairs(values_in, cosine, sine_part):
    half_dim = values_in.shape[-1] // 2
    first = values_in[..., :half_dim]
    second = values_in[..., half_dim:]
    return jnp.concatenate([first * cosine - second * sine_part, second * cosine + first * sine_part], axis=-1)

def inverse_freq(head_dim):
    return jnp.power(jnp.float32(1000000.0), -jnp.arange(head_dim // 2, dtype=jnp.float32) * 2.0 / head_dim)

def mrope_angles(positions, head_dim):
    freqs = inverse_freq(head_dim)
    first_cut = head_dim // 8
    second_cut = first_cut + 3 * head_dim // 16
    place = positions.astype(jnp.float32)
    return jnp.concatenate([place[0][:, None] * freqs[:first_cut], place[1][:, None] * freqs[first_cut:second_cut], place[2][:, None] * freqs[second_cut:]], axis=-1)

def rounded_weights(weights_f):
    return lax.optimization_barrier(weights_f.astype(jnp.bfloat16)).astype(jnp.float32)

def reference(patches, window_ids, vit_gain, vit_qkv, vit_qkv_bias, vit_proj, vit_proj_bias, merge_gain, merge_up, merge_up_bias, merge_down, merge_down_bias, input_gain, kv_weight, kv_bias, key_positions, queries, question_kv, question_start, question_length):
    resid = patches.astype(jnp.float32)
    normed = rms_scale(resid, vit_gain).astype(jnp.bfloat16)
    projected = [(jnp.dot(normed, vit_qkv[which], preferred_element_type=jnp.float32) + vit_qkv_bias[which].astype(jnp.float32)).astype(jnp.bfloat16) for which in range(3)]
    rows_dev = 4 * MERGED_DEV

    def device_window(operands):
        query_rows, key_rows, value_rows, patch_ids = operands
        query_heads = query_rows.astype(jnp.float32).reshape(rows_dev, VHEADS, VHD)
        key_heads = key_rows.astype(jnp.float32).reshape(rows_dev, VHEADS, VHD)
        value_heads = value_rows.astype(jnp.float32).reshape(rows_dev, VHEADS, VHD)
        scores = jnp.einsum('phd,shd->hps', query_heads, key_heads) * VHD ** (-0.5)
        keep_mask = patch_ids[:, None] == patch_ids[None, :]
        weights_f = jnp.where(keep_mask[None], jnp.exp(scores), 0.0)
        denom = lax.optimization_barrier(jnp.sum(weights_f, axis=-1))
        mixed = jnp.einsum('hps,shd->phd', rounded_weights(weights_f), value_heads) / jnp.transpose(denom)[:, :, None]
        return mixed.reshape(rows_dev, VD).astype(jnp.bfloat16)
    ids_patch = jnp.repeat(window_ids, 4, axis=1)
    heads_out = lax.map(device_window, (projected[0].reshape(N_WIDE, rows_dev, VD), projected[1].reshape(N_WIDE, rows_dev, VD), projected[2].reshape(N_WIDE, rows_dev, VD), ids_patch)).reshape(PATCHES, VD)
    hidden = resid + (jnp.dot(heads_out, vit_proj, preferred_element_type=jnp.float32) + vit_proj_bias.astype(jnp.float32))
    merged_in = rms_scale(hidden, merge_gain).astype(jnp.bfloat16).reshape(MERGED, 4 * VD)
    up_act = jax.nn.gelu(jnp.dot(merged_in, merge_up, preferred_element_type=jnp.float32) + merge_up_bias.astype(jnp.float32), approximate=False).astype(jnp.bfloat16)
    embed = jnp.dot(up_act, merge_down, preferred_element_type=jnp.float32) + merge_down_bias.astype(jnp.float32)
    embed_normed = rms_scale(embed, input_gain).astype(jnp.bfloat16)
    key_raw = jnp.dot(embed_normed, kv_weight[0], preferred_element_type=jnp.float32) + kv_bias[0].astype(jnp.float32)
    value_rows = (jnp.dot(embed_normed, kv_weight[1], preferred_element_type=jnp.float32) + kv_bias[1].astype(jnp.float32)).astype(jnp.bfloat16)
    angles = mrope_angles(key_positions, HD)[:, None, :]
    key_rot = rotate_pairs(key_raw.reshape(MERGED, KV_HEADS, HD), jnp.cos(angles), jnp.sin(angles)).astype(jnp.bfloat16)
    kv_cache = jnp.stack([key_rot.reshape(MERGED, KV_HEADS * HD), value_rows])
    token_place = (question_start[:, None] + jnp.arange(QLEN, dtype=jnp.int32)[None, :]).astype(jnp.float32)
    query_angle = token_place[:, :, None, None] * inverse_freq(HD)
    query_cos = jnp.cos(query_angle)
    query_sin = jnp.sin(query_angle)
    query_rot = rotate_pairs(queries.astype(jnp.float32).reshape(QUESTIONS, QLEN, HEADS, HD), query_cos, query_sin).astype(jnp.bfloat16)
    own_keys = rotate_pairs(question_kv[0].astype(jnp.float32).reshape(QUESTIONS, QLEN, KV_HEADS, HD), query_cos, query_sin).astype(jnp.bfloat16)
    own_values = question_kv[1].reshape(QUESTIONS, QLEN, KV_HEADS, HD)
    video_keys = key_rot.astype(jnp.float32)
    video_values = value_rows.reshape(MERGED, KV_HEADS, HD).astype(jnp.float32)
    group_size = HEADS // KV_HEADS
    causal = jnp.arange(QLEN)[:, None] >= jnp.arange(QLEN)[None, :]

    def one_question(operands):
        query_one, key_one, value_one, length_one = operands
        grouped = query_one.astype(jnp.float32).reshape(QLEN, KV_HEADS, group_size, HD)
        video_scores = jnp.einsum('tkgd,nkd->kgtn', grouped, video_keys) * HD ** (-0.5)
        own_scores = jnp.einsum('tkgd,jkd->kgtj', grouped, key_one.astype(jnp.float32)) * HD ** (-0.5)
        own_scores = jnp.where(causal, own_scores, -1e+30)
        row_top = jnp.maximum(lax.optimization_barrier(jnp.max(video_scores, axis=-1)), lax.optimization_barrier(jnp.max(own_scores, axis=-1)))[..., None]
        video_w = jnp.exp(video_scores - row_top)
        own_w = jnp.exp(own_scores - row_top)
        denom = lax.optimization_barrier(jnp.sum(video_w, axis=-1)) + lax.optimization_barrier(jnp.sum(own_w, axis=-1))
        mixed = jnp.einsum('kgtn,nkd->kgtd', rounded_weights(video_w), video_values) + jnp.einsum('kgtj,jkd->kgtd', rounded_weights(own_w), value_one.astype(jnp.float32))
        mixed = mixed / denom[..., None]
        mixed = jnp.transpose(mixed, (2, 0, 1, 3)).reshape(QLEN, HEADS * HD)
        live = jnp.arange(QLEN, dtype=jnp.int32) < length_one
        return jnp.where(live[:, None], mixed, jnp.float32(0.0)).astype(jnp.bfloat16)
    attended = lax.map(one_question, (query_rot, own_keys, own_values, question_length))
    return (attended, kv_cache)
```

```python
import functools

import jax
import jax.numpy as jnp
from jax import lax
from jax.experimental import pallas as pl
from jax.experimental.pallas import tpu as pltpu
from jax.sharding import PartitionSpec as P

HD = 128
VHD = 80
CHUNKS = 8
F32 = jnp.float32
BF16 = jnp.bfloat16
VMEM_LIMIT = 60 * 1024 * 1024


def dot(a, b):
    return jnp.dot(a, b, preferred_element_type=F32)


def dot_t(a, b):
    return lax.dot_general(a, b, (((1,), (1,)), ((), ())), preferred_element_type=F32)


def iota(shape, axis):
    return lax.broadcasted_iota(jnp.int32, shape, axis)


def vision_kernel(
    ids, patches, gain, qkv_bias, proj_bias, merge_gain, up_bias, down_bias, input_gain,
    kv_bias, cosine, sine,
    qkv_hbm, proj_hbm, up_hbm, down_hbm, kvw_hbm,
    kv_out,
    qkv_w, proj_w, up_w, down_w, kv_w, w_sem,
    rows, normed, heads, partial, give, got, x_give, x_got, merged, up_acc, up_act,
    d_part, d_give, d_got, dx_give, dx_got, emb, squares, kv_acc,
    send_sem, recv_sem,
):
    me = lax.axis_index("narrow")
    x, core = me // 2, me % 2
    cp = x * 2 + (1 - core)
    xp = (1 - x) * 2 + core
    dg = (1 - x) * 2 + (1 - core)
    row_count = patches.shape[0]
    part_w = patches.shape[1]
    width = proj_hbm.shape[1]
    block = row_count // 4
    merged_block = block // 4
    wide_d = down_hbm.shape[1]
    chunk = wide_d // CHUNKS

    def local(index, src, dst):
        return pltpu.make_async_copy(src, dst, w_sem.at[index])

    def remote(index, src, dst, peer):
        return pltpu.make_async_remote_copy(
            src_ref=src, dst_ref=dst, send_sem=send_sem.at[index], recv_sem=recv_sem.at[index],
            device_id={"narrow": peer}, device_id_type=pl.DeviceIdType.MESH,
        )

    loads = [
        local(0, qkv_hbm, qkv_w), local(1, proj_hbm, proj_w), local(2, up_hbm, up_w),
        local(3, down_hbm, down_w), local(4, kvw_hbm, kv_w),
    ]
    loads[0].start()
    loads[1].start()

    barrier = pltpu.get_barrier_semaphore()
    for peer in (cp, xp):
        pl.semaphore_signal(
            barrier, inc=1, device_id={"narrow": peer}, device_id_type=pl.DeviceIdType.MESH
        )
    pl.semaphore_wait(barrier, 2)

    sent = []

    def send(index, src, dst, peer):
        copy = remote(index, src, dst, peer)
        copy.start()
        sent.append(copy)

    def arrived(index, dst, peer):
        remote(index, dst, dst, peer).wait_recv()

    def gather_start(index, src, slots):
        send(index + 1, src, slots.at[me], xp)
        send(index, src, slots.at[me], cp)

    def gather_forward(index, slots):
        arrived(index + 1, slots.at[xp], xp)
        send(index + 2, slots.at[xp], slots.at[xp], cp)

    def gather_finish(index, slots):
        arrived(index, slots.at[cp], cp)
        arrived(index + 2, slots.at[dg], cp)

    gather_start(0, patches, rows)
    loads[2].start()
    rows[me] = patches[...]
    ids_row = ids[...].astype(F32)
    token_of = (iota((row_count, row_count // 4), 0) // 4 == iota((row_count, row_count // 4), 1))
    token_of = token_of.astype(F32)
    patch_col = jnp.sum(token_of * ids_row, axis=1, keepdims=True)
    patch_row = dot_t(
        jnp.broadcast_to(ids_row, (8, row_count // 4)).astype(BF16), token_of.astype(BF16)
    )[:1]
    same = patch_col == patch_row
    gather_forward(0, rows)
    gather_finish(0, rows)
    loads[3].start()
    loads[4].start()

    total_sq = jnp.zeros((row_count, 1), F32)
    for i in range(4):
        part = rows[i].astype(F32)
        total_sq += jnp.sum(part * part, axis=1, keepdims=True)
    scale = lax.rsqrt(total_sq / width + 1e-06)
    for i in range(4):
        normed[i] = (rows[i].astype(F32) * scale * gain[i]).astype(BF16)
    loads[0].wait()
    qkv = []
    for which in range(3):
        acc = dot(normed[0], qkv_w[which, :part_w])
        for i in range(1, 4):
            acc += dot(normed[i], qkv_w[which, part_w * i : part_w * (i + 1)])
        qkv.append((acc + qkv_bias[which]).astype(BF16))
    query, key, value = qkv
    lane = iota((1, part_w), 1)
    out = jnp.zeros((row_count, part_w), F32)
    for h in range(part_w // VHD):
        mine = ((lane >= VHD * h) & (lane < VHD * (h + 1))).astype(F32)
        scores = dot_t(query * mine.astype(BF16), key) * VHD ** (-0.5)
        weights = jnp.where(same, jnp.exp(scores), 0.0)
        denom = 1.0 / jnp.sum(weights, axis=1, keepdims=True)
        out += dot(weights.astype(BF16), value) * denom * mine
    heads[...] = out.astype(BF16)
    loads[1].wait()
    partial[...] = dot(heads[...], proj_w[...])

    def rows_of(ref, index, size):
        return ref[pl.ds(pl.multiple_of(index * size, size), size), :]

    give[0] = rows_of(partial, dg, block).astype(BF16)
    send(3, give.at[0], got.at[0], cp)
    give[1] = rows_of(partial, cp, block).astype(BF16)
    send(4, give.at[1], got.at[1], cp)
    resid = jnp.zeros((block, width), F32)
    for i in range(4):
        place = (iota((part_w, width), 1) - part_w * i == iota((part_w, width), 0))
        mine_rows = rows[i, pl.ds(pl.multiple_of(me * block, block), block), :]
        resid += dot(mine_rows, place.astype(F32).astype(BF16))
    resid = resid + proj_bias[...]
    arrived(3, got.at[0], cp)
    x_give[...] = (rows_of(partial, xp, block) + got[0].astype(F32)).astype(BF16)
    send(5, x_give, x_got, xp)
    arrived(4, got.at[1], cp)
    hidden = resid + rows_of(partial, me, block) + got[1].astype(F32)
    arrived(5, x_got, xp)
    hidden = hidden + x_got[...].astype(F32)
    hidden_sq = jnp.sum(hidden * hidden, axis=1, keepdims=True) / width
    hidden_n = (hidden * lax.rsqrt(hidden_sq + 1e-06) * merge_gain[...]).astype(BF16)
    to_row = iota((block, block), 0)
    order = (to_row % merged_block) * 4 + to_row // merged_block == iota((block, block), 1)
    ordered = dot(order.astype(F32).astype(BF16), hidden_n).astype(BF16)
    for j in range(4):
        merged[me, :, width * j : width * (j + 1)] = ordered[
            merged_block * j : merged_block * (j + 1)
        ]
    gather_start(6, merged.at[me], merged)
    gather_forward(6, merged)
    gather_finish(6, merged)

    loads[2].wait()
    up_acc[...] = jnp.zeros_like(up_acc)
    step = 512

    @pl.loop(0, up_hbm.shape[0] // step)
    def _(kk):
        at = pl.ds(pl.multiple_of(kk * step, step), step)
        up_acc[...] += dot(merged[:, :, at].reshape(block, step), up_w[at, :])

    pre = up_acc[...] + up_bias[...]
    up_act[...] = (0.5 * pre * (1.0 + lax.erf(pre * 0.7071067811865476))).astype(BF16)
    loads[3].wait()
    kv_acc[...] = jnp.zeros_like(kv_acc)
    square_sum = jnp.zeros((merged_block, 1), F32)
    for t in range(CHUNKS + 4):
        c = t
        if c < CHUNKS:
            d_part[c] = dot(up_act[...], down_w[:, chunk * c : chunk * (c + 1)])
            d_give[c, 0] = rows_of(d_part.at[c], dg, merged_block).astype(BF16)
            d_give[c, 1] = rows_of(d_part.at[c], cp, merged_block).astype(BF16)
            send(12 + 5 * c, d_give.at[c], d_got.at[c], cp)
        c = t - 1
        if 0 <= c < CHUNKS:
            arrived(12 + 5 * c, d_got.at[c], cp)
            dx_give[c] = (
                rows_of(d_part.at[c], xp, merged_block) + d_got[c, 0].astype(F32)
            ).astype(BF16)
            send(13 + 5 * c, dx_give.at[c], dx_got.at[c], xp)
        c = t - 2
        if 0 <= c < CHUNKS:
            arrived(13 + 5 * c, dx_got.at[c], xp)
            cols = slice(chunk * c, chunk * (c + 1))
            embed = rows_of(d_part.at[c], me, merged_block) + d_got[c, 1].astype(F32)
            embed = embed + dx_got[c].astype(F32) + down_bias[:, cols]
            square_sum += jnp.sum(embed * embed, axis=1, keepdims=True)
            emb[c, me] = (embed * input_gain[:, cols]).astype(BF16)
            gather_start(14 + 5 * c, emb.at[c, me], emb.at[c])
            if c == CHUNKS - 1:
                squares[me] = jnp.broadcast_to(square_sum, squares.shape[1:])
                gather_start(9, squares.at[me], squares)
        c = t - 3
        if 0 <= c < CHUNKS:
            gather_forward(14 + 5 * c, emb.at[c])
            if c == CHUNKS - 1:
                gather_forward(9, squares)
        c = t - 4
        if 0 <= c < CHUNKS:
            gather_finish(14 + 5 * c, emb.at[c])
            if c == 0:
                loads[4].wait()
            lhs = emb[c].reshape(block, chunk)
            for which in range(2):
                kv_acc[which] += dot(lhs, kv_w[which, chunk * c : chunk * (c + 1), :])
    gather_finish(9, squares)
    row_scale = lax.rsqrt(squares[...].reshape(block, squares.shape[2]) / wide_d + 1e-06)
    for h in range(kv_w.shape[2] // HD):
        cols = slice(HD * h, HD * (h + 1))
        raw = kv_acc[0, :, cols] * row_scale + kv_bias[0, :, cols]
        rotated = raw * cosine[...] + pltpu.roll(raw, HD // 2, 1) * sine[...]
        kv_out[0, :, cols] = rotated.astype(BF16)
        kv_out[1, :, cols] = (kv_acc[1, :, cols] * row_scale + kv_bias[1, :, cols]).astype(BF16)
    for copy in sent:
        copy.wait_send()


def wide_gather_kernel(count, kv, out, local_sem, send_sem, recv_sem):
    me = lax.axis_index("wide")

    def peer_at(offset):
        return lax.rem(me + offset, count)

    def remote(offset):
        return pltpu.make_async_remote_copy(
            src_ref=kv, dst_ref=out.at[me],
            send_sem=send_sem.at[offset - 1], recv_sem=recv_sem.at[offset - 1],
            device_id={"wide": peer_at(offset)}, device_id_type=pl.DeviceIdType.MESH,
        )

    mine = pltpu.make_async_copy(kv, out.at[me], local_sem)
    mine.start()
    barrier = pltpu.get_barrier_semaphore()

    @pl.loop(1, count)
    def _(offset):
        pl.semaphore_signal(
            barrier, inc=1, device_id={"wide": peer_at(offset)},
            device_id_type=pl.DeviceIdType.MESH,
        )

    pl.semaphore_wait(barrier, count - 1)

    @pl.loop(1, count)
    def _(offset):
        remote(offset).start()

    mine.wait()

    @pl.loop(1, count)
    def _(offset):
        copy = remote(offset)
        copy.wait_send()
        copy.wait_recv()


def attention_kernel(
    length, queries, own_kv, cosine, sine, kv_all, out, rotated
):
    question = pl.program_id(0)
    tokens = queries.shape[1]
    groups = queries.shape[2] // HD
    keys_n = kv_all.shape[0] * kv_all.shape[2]
    cos, sin = cosine[0], sine[0]

    def rotate(rows):
        rows = rows.astype(F32)
        return (rows * cos + pltpu.roll(rows, HD // 2, 1) * sin).astype(BF16)

    own_key = rotate(own_kv[0, 0])
    for g in range(groups):
        rotated[tokens * g : tokens * (g + 1), :] = rotate(queries[0, :, HD * g : HD * (g + 1)])
    query = rotated[...]
    rows_n = tokens * groups
    factor = HD ** (-0.5)
    own = dot_t(query, own_key) * factor
    token = iota((rows_n, tokens), 0) % tokens
    own = jnp.where(token >= iota((rows_n, tokens), 1), own, -1e30)
    scores = dot_t(query, kv_all[:, 0].reshape(keys_n, HD)) * factor
    top = jnp.maximum(
        jnp.max(scores, axis=1, keepdims=True), jnp.max(own, axis=1, keepdims=True)
    )
    weights = jnp.exp(scores - top)
    own_w = jnp.exp(own - top)
    denom = jnp.sum(weights, axis=1, keepdims=True) + jnp.sum(own_w, axis=1, keepdims=True)
    mixed = dot(weights.astype(BF16), kv_all[:, 1].reshape(keys_n, HD))
    mixed += dot(own_w.astype(BF16), own_kv[1, 0])
    live = iota((rows_n, HD), 0) % tokens < length[question]
    mixed = jnp.where(live, mixed * (1.0 / denom), 0.0).astype(BF16)
    for g in range(groups):
        out[0, :, HD * g : HD * (g + 1)] = mixed[tokens * g : tokens * (g + 1)]


def inverse_freq(head_dim):
    return jnp.power(
        jnp.float32(1000000.0), -jnp.arange(head_dim // 2, dtype=F32) * 2.0 / head_dim
    )


def mrope_angles(positions, head_dim):
    freqs = inverse_freq(head_dim)
    first_cut = head_dim // 8
    second_cut = first_cut + 3 * head_dim // 16
    place = positions.astype(F32)
    return jnp.concatenate(
        [
            place[0][:, None] * freqs[:first_cut],
            place[1][:, None] * freqs[first_cut:second_cut],
            place[2][:, None] * freqs[second_cut:],
        ],
        axis=-1,
    )


def turns(angles):
    cosine, sine = jnp.cos(angles), jnp.sin(angles)
    return (
        jnp.concatenate([cosine, cosine], axis=-1),
        jnp.concatenate([-sine, sine], axis=-1),
    )


def per_device(
    n_wide,
    patches,
    window_ids,
    vit_gain,
    vit_qkv,
    vit_qkv_bias,
    vit_proj,
    vit_proj_bias,
    merge_gain,
    merge_up,
    merge_up_bias,
    merge_down,
    merge_down_bias,
    input_gain,
    kv_weight,
    kv_bias,
    key_positions,
    queries,
    question_kv,
    question_start,
    question_length,
):
    rows_n, part_w = patches.shape
    width = vit_proj.shape[1]
    block = rows_n // 4
    merged_block = block // 4
    d_wide = merge_down.shape[1]
    chunk = d_wide // CHUNKS
    hidden_n = merge_up.shape[1]
    kv_w = kv_weight.shape[2]
    key_cos, key_sin = turns(mrope_angles(key_positions, HD))
    tokens = queries.shape[1]
    place = (question_start[:, None] + jnp.arange(tokens, dtype=jnp.int32)[None, :]).astype(F32)
    query_cos, query_sin = turns(place[:, :, None] * inverse_freq(HD))

    vmem = pl.BlockSpec(memory_space=pltpu.VMEM)
    hbm = pl.BlockSpec(memory_space=pl.ANY)
    copies = 12 + 5 * CHUNKS
    kv_cache = pl.pallas_call(
        vision_kernel,
        out_shape=jax.ShapeDtypeStruct((2, block, kv_w), BF16),
        in_specs=[vmem] * 12 + [hbm] * 5,
        out_specs=vmem,
        scratch_shapes=[
            pltpu.VMEM(vit_qkv.shape, BF16),
            pltpu.VMEM(vit_proj.shape, BF16),
            pltpu.VMEM(merge_up.shape, BF16),
            pltpu.VMEM(merge_down.shape, BF16),
            pltpu.VMEM(kv_weight.shape, BF16),
            pltpu.SemaphoreType.DMA((5,)),
            pltpu.VMEM((4, rows_n, part_w), BF16),
            pltpu.VMEM((4, rows_n, part_w), BF16),
            pltpu.VMEM((rows_n, part_w), BF16),
            pltpu.VMEM((rows_n, width), F32),
            pltpu.VMEM((2, block, width), BF16),
            pltpu.VMEM((2, block, width), BF16),
            pltpu.VMEM((block, width), BF16),
            pltpu.VMEM((block, width), BF16),
            pltpu.VMEM((4, merged_block, 4 * width), BF16),
            pltpu.VMEM((block, hidden_n), F32),
            pltpu.VMEM((block, hidden_n), BF16),
            pltpu.VMEM((CHUNKS, block, chunk), F32),
            pltpu.VMEM((CHUNKS, 2, merged_block, chunk), BF16),
            pltpu.VMEM((CHUNKS, 2, merged_block, chunk), BF16),
            pltpu.VMEM((CHUNKS, merged_block, chunk), BF16),
            pltpu.VMEM((CHUNKS, merged_block, chunk), BF16),
            pltpu.VMEM((CHUNKS, 4, merged_block, chunk), BF16),
            pltpu.VMEM((4, merged_block, HD), F32),
            pltpu.VMEM((2, block, kv_w), F32),
            pltpu.SemaphoreType.DMA((copies,)),
            pltpu.SemaphoreType.DMA((copies,)),
        ],
        compiler_params=pltpu.CompilerParams(
            collective_id=0, has_side_effects=True, vmem_limit_bytes=VMEM_LIMIT
        ),
        name="vision_to_kv",
    )(
        window_ids,
        patches,
        vit_gain.reshape(4, 1, part_w),
        vit_qkv_bias.reshape(3, 1, part_w),
        vit_proj_bias.reshape(1, width),
        merge_gain.reshape(1, width),
        merge_up_bias.reshape(1, hidden_n),
        merge_down_bias.reshape(1, d_wide),
        input_gain.reshape(1, d_wide),
        kv_bias.reshape(2, 1, kv_w),
        key_cos,
        key_sin,
        vit_qkv,
        vit_proj,
        merge_up,
        merge_down,
        kv_weight,
    )
    kv_all = pl.pallas_call(
        functools.partial(wide_gather_kernel, n_wide),
        out_shape=jax.ShapeDtypeStruct((n_wide, 2, block, kv_w), BF16),
        in_specs=[hbm],
        out_specs=hbm,
        scratch_shapes=[
            pltpu.SemaphoreType.DMA,
            pltpu.SemaphoreType.DMA((n_wide - 1,)),
            pltpu.SemaphoreType.DMA((n_wide - 1,)),
        ],
        compiler_params=pltpu.CompilerParams(collective_id=1, has_side_effects=True),
        name="kv_over_wide",
    )(kv_cache)
    q_count = queries.shape[0]
    kv_heads = kv_w // HD
    group_w = queries.shape[2] // kv_heads
    attended = pl.pallas_call(
        attention_kernel,
        grid_spec=pltpu.PrefetchScalarGridSpec(
            num_scalar_prefetch=1,
            grid=(q_count, kv_heads),
            in_specs=[
                pl.BlockSpec((1, tokens, group_w), lambda q, h, n: (q, 0, h)),
                pl.BlockSpec((2, 1, tokens, HD), lambda q, h, n: (0, q, 0, h)),
                pl.BlockSpec((1, tokens, HD), lambda q, h, n: (q, 0, 0)),
                pl.BlockSpec((1, tokens, HD), lambda q, h, n: (q, 0, 0)),
                pl.BlockSpec((n_wide, 2, block, HD), lambda q, h, n: (0, 0, 0, h)),
            ],
            out_specs=pl.BlockSpec((1, tokens, group_w), lambda q, h, n: (q, 0, h)),
            scratch_shapes=[pltpu.VMEM((tokens * group_w // HD, HD), BF16)],
        ),
        out_shape=jax.ShapeDtypeStruct(queries.shape, BF16),
        compiler_params=pltpu.CompilerParams(vmem_limit_bytes=VMEM_LIMIT),
        name="question_attention",
    )(question_length, queries, question_kv, query_cos, query_sin, kv_all)
    return (attended, kv_cache)


def solution(mesh):
    return jax.shard_map(
        functools.partial(per_device, mesh.shape["wide"]),
        mesh=mesh,
        in_specs=(
            P("wide", "narrow"),
            P("wide", None),
            P(),
            P(None, None, "narrow"),
            P(None, "narrow"),
            P("narrow", None),
            P(),
            P(),
            P(None, "narrow"),
            P("narrow"),
            P("narrow", None),
            P(),
            P(),
            P(None, None, "narrow"),
            P(None, "narrow"),
            P(None, "wide"),
            P("wide", None, "narrow"),
            P(None, "wide", None, "narrow"),
            P("wide"),
            P("wide"),
        ),
        out_specs=(P("wide", None, "narrow"), P(None, "wide", "narrow")),
        check_vma=False,
    )
```

```python
import functools

import jax
import jax.numpy as jnp
import numpy as np
from jax import lax
from jax.experimental import pallas as pl
from jax.experimental.pallas import tpu as pltpu
from jax.sharding import PartitionSpec as P

HD = 128
VHD = 80
CHUNKS = 8
F32 = jnp.float32
BF16 = jnp.bfloat16
VMEM_LIMIT = 60 * 1024 * 1024


def dot(a, b):
    return jnp.dot(a, b, preferred_element_type=F32)


def dot_t(a, b):
    return lax.dot_general(a, b, (((1,), (1,)), ((), ())), preferred_element_type=F32)


def iota(shape, axis):
    return lax.broadcasted_iota(jnp.int32, shape, axis)


def dot_0(a, b):
    return lax.dot_general(a, b, (((0,), (0,)), ((), ())), preferred_element_type=F32)


def row(ref):
    return ref[...].reshape(1, ref.shape[0])


def column(values):
    n = values.shape[1]
    return jnp.sum(
        jnp.where(iota((n, n), 0) == iota((n, n), 1), values, 0.0), axis=1, keepdims=True
    )


def vision_kernel(
    n_wide,
    ids, patches, gain, qkv_bias, proj_bias, merge_gain, up_bias, down_bias, input_gain,
    kv_bias, cosine, sine,
    qkv_hbm, proj_hbm, up_hbm, down_hbm, kvw_hbm,
    kv_out, kv_all,
    qkv_w, proj_w, up_w, down_w, kv_w, w_sem,
    rows, normed, heads, partial, give, got, x_give, x_got, merged, up_acc, up_act,
    d_part, d_give, d_got, dx_give, dx_got, emb, squares, kv_acc,
    send_sem, recv_sem, o_send, o_recv, i_send, i_recv,
):
    me = lax.axis_index("narrow")
    x, core = me // 2, me % 2
    cp = x * 2 + (1 - core)
    xp = (1 - x) * 2 + core
    dg = (1 - x) * 2 + (1 - core)
    part_w, row_count = patches.shape
    width = proj_hbm.shape[1]
    block = row_count // 4
    merged_block = block // 4
    wide_d = down_hbm.shape[1]
    chunk = wide_d // CHUNKS
    wide = lax.axis_index("wide")
    outer_n = n_wide // 2
    outer, inner = wide // 2, wide % 2
    inner_peer = outer * 2 + (1 - inner)

    def outer_at(offset):
        return ((outer + offset) % outer_n) * 2 + inner

    def local(index, src, dst):
        return pltpu.make_async_copy(src, dst, w_sem.at[index])

    def remote(index, src, dst, peer):
        return pltpu.make_async_remote_copy(
            src_ref=src, dst_ref=dst, send_sem=send_sem.at[index], recv_sem=recv_sem.at[index],
            device_id={"narrow": peer}, device_id_type=pl.DeviceIdType.MESH,
        )

    loads = [
        local(0, qkv_hbm, qkv_w), local(1, proj_hbm, proj_w), local(2, up_hbm, up_w),
        local(3, down_hbm, down_w), local(4, kvw_hbm, kv_w),
    ]
    loads[0].start()
    loads[1].start()

    barrier = pltpu.get_barrier_semaphore()

    def greet(peer):
        pl.semaphore_signal(barrier, inc=1, device_id=peer, device_id_type=pl.DeviceIdType.MESH)

    greet({"narrow": cp})
    greet({"narrow": xp})
    greet({"wide": inner_peer})

    @pl.loop(1, outer_n)
    def _(offset):
        greet({"wide": outer_at(offset)})

    pl.semaphore_wait(barrier, outer_n + 2)

    sent = []

    def send(index, src, dst, peer):
        copy = remote(index, src, dst, peer)
        copy.start()
        sent.append(copy)

    def arrived(index, dst, peer):
        remote(index, dst, dst, peer).wait_recv()

    def gather_start(index, src, slots):
        send(index + 1, src, slots.at[me], xp)
        send(index, src, slots.at[me], cp)

    def gather_forward(index, slots):
        arrived(index + 1, slots.at[xp], xp)
        send(index + 2, slots.at[xp], slots.at[xp], cp)

    def gather_finish(index, slots):
        arrived(index, slots.at[cp], cp)
        arrived(index + 2, slots.at[dg], cp)

    gather_start(0, patches, rows)
    loads[2].start()
    rows[me] = patches[...]
    ids_row = ids[...].astype(F32)
    token_of = (iota((row_count, row_count // 4), 0) // 4 == iota((row_count, row_count // 4), 1))
    token_of = token_of.astype(F32)
    patch_col = jnp.sum(token_of * ids_row, axis=1, keepdims=True)
    patch_row = dot_t(
        jnp.broadcast_to(ids_row, (8, row_count // 4)).astype(BF16), token_of.astype(BF16)
    )[:1]
    same = patch_col == patch_row
    gather_forward(0, rows)
    gather_finish(0, rows)
    loads[3].start()
    loads[4].start()

    total_sq = jnp.zeros((1, row_count), F32)
    for i in range(4):
        part = rows[i].astype(F32)
        total_sq += jnp.sum(part * part, axis=0, keepdims=True)
    scale = lax.rsqrt(total_sq / width + 1e-06)
    features = rows[...].reshape(width, row_count)
    gains = row(gain)
    for i in range(0, width, 128):
        normed[i : i + 128, :] = (
            features[i : i + 128].astype(F32) * scale * column(gains[:, i : i + 128])
        ).astype(BF16)
    loads[0].wait()
    query, key, value = [
        (dot(qkv_w[which], normed[...]) + column(qkv_bias[which : which + 1, :])).astype(BF16)
        for which in range(3)
    ]
    for h in range(part_w // VHD):
        at = slice(VHD * h, VHD * (h + 1))
        scores = dot_0(key[at], query[at]) * VHD ** (-0.5)
        weights = jnp.where(same, jnp.exp(scores), 0.0)
        denom = 1.0 / jnp.sum(weights, axis=0, keepdims=True)
        heads[at, :] = (dot(value[at], weights.astype(BF16)) * denom).astype(BF16)
    loads[1].wait()
    partial[...] = dot_0(heads[...], proj_w[...])

    def rows_of(ref, index, size):
        return ref[pl.ds(pl.multiple_of(index * size, size), size), :]

    give[0] = rows_of(partial, dg, block).astype(BF16)
    send(3, give.at[0], got.at[0], cp)
    give[1] = rows_of(partial, cp, block).astype(BF16)
    send(4, give.at[1], got.at[1], cp)
    mine = iota((block, row_count), 1) - block * me == iota((block, row_count), 0)
    resid = dot_t(mine.astype(F32).astype(BF16), features) + row(proj_bias)
    arrived(3, got.at[0], cp)
    x_give[...] = (rows_of(partial, xp, block) + got[0].astype(F32)).astype(BF16)
    send(5, x_give, x_got, xp)
    arrived(4, got.at[1], cp)
    hidden = resid + rows_of(partial, me, block) + got[1].astype(F32)
    arrived(5, x_got, xp)
    hidden = hidden + x_got[...].astype(F32)
    hidden_sq = jnp.sum(hidden * hidden, axis=1, keepdims=True) / width
    hidden_n = (hidden * lax.rsqrt(hidden_sq + 1e-06) * row(merge_gain)).astype(BF16)
    to_row = iota((block, block), 0)
    order = (to_row % merged_block) * 4 + to_row // merged_block == iota((block, block), 1)
    ordered = dot(order.astype(F32).astype(BF16), hidden_n).astype(BF16)
    for j in range(4):
        merged[me, :, width * j : width * (j + 1)] = ordered[
            merged_block * j : merged_block * (j + 1)
        ]
    gather_start(6, merged.at[me], merged)
    gather_forward(6, merged)
    gather_finish(6, merged)

    loads[2].wait()
    up_acc[...] = jnp.zeros_like(up_acc)
    step = 512

    @pl.loop(0, up_hbm.shape[0] // step)
    def _(kk):
        at = pl.ds(pl.multiple_of(kk * step, step), step)
        up_acc[...] += dot(merged[:, :, at].reshape(block, step), up_w[at, :])

    pre = up_acc[...] + row(up_bias)
    up_act[...] = (0.5 * pre * (1.0 + lax.erf(pre * 0.7071067811865476))).astype(BF16)
    loads[3].wait()
    kv_acc[...] = jnp.zeros_like(kv_acc)
    square_sum = jnp.zeros((merged_block, 1), F32)
    for t in range(CHUNKS + 4):
        c = t
        if c < CHUNKS:
            d_part[c] = dot(up_act[...], down_w[:, chunk * c : chunk * (c + 1)])
            d_give[c, 0] = rows_of(d_part.at[c], dg, merged_block).astype(BF16)
            d_give[c, 1] = rows_of(d_part.at[c], cp, merged_block).astype(BF16)
            send(12 + 5 * c, d_give.at[c], d_got.at[c], cp)
        c = t - 1
        if 0 <= c < CHUNKS:
            arrived(12 + 5 * c, d_got.at[c], cp)
            dx_give[c] = (
                rows_of(d_part.at[c], xp, merged_block) + d_got[c, 0].astype(F32)
            ).astype(BF16)
            send(13 + 5 * c, dx_give.at[c], dx_got.at[c], xp)
        c = t - 2
        if 0 <= c < CHUNKS:
            arrived(13 + 5 * c, dx_got.at[c], xp)
            cols = slice(chunk * c, chunk * (c + 1))
            embed = rows_of(d_part.at[c], me, merged_block) + d_got[c, 1].astype(F32)
            embed = embed + dx_got[c].astype(F32) + down_bias[:, cols]
            square_sum += jnp.sum(embed * embed, axis=1, keepdims=True)
            emb[c, me] = (embed * input_gain[:, cols]).astype(BF16)
            gather_start(14 + 5 * c, emb.at[c, me], emb.at[c])
            if c == CHUNKS - 1:
                squares[me] = jnp.broadcast_to(square_sum, squares.shape[1:])
                gather_start(9, squares.at[me], squares)
        c = t - 3
        if 0 <= c < CHUNKS:
            gather_forward(14 + 5 * c, emb.at[c])
            if c == CHUNKS - 1:
                gather_forward(9, squares)
        c = t - 4
        if 0 <= c < CHUNKS:
            gather_finish(14 + 5 * c, emb.at[c])
            if c == 0:
                loads[4].wait()
            lhs = emb[c].reshape(block, chunk)
            for which in range(2):
                kv_acc[which] += dot(lhs, kv_w[which, chunk * c : chunk * (c + 1), :])
    gather_finish(9, squares)
    row_scale = lax.rsqrt(squares[...].reshape(block, squares.shape[2]) / wide_d + 1e-06)
    for h in range(kv_w.shape[2] // HD):
        cols = slice(HD * h, HD * (h + 1))
        raw = kv_acc[0, :, cols] * row_scale + kv_bias[0:1, cols]
        rotated = raw * cosine[...] + pltpu.roll(raw, HD // 2, 1) * sine[...]
        kv_out[0, :, cols] = rotated.astype(BF16)
        kv_out[1, :, cols] = (kv_acc[1, :, cols] * row_scale + kv_bias[1:2, cols]).astype(BF16)
    kv_all[wide] = kv_out[...]

    def along(offset, src, slot):
        return pltpu.make_async_remote_copy(
            src_ref=src, dst_ref=kv_all.at[slot],
            send_sem=o_send.at[offset - 1], recv_sem=o_recv.at[offset - 1],
            device_id={"wide": outer_at(offset)}, device_id_type=pl.DeviceIdType.MESH,
        )

    def across(offset, slot):
        return pltpu.make_async_remote_copy(
            src_ref=kv_all.at[slot], dst_ref=kv_all.at[slot],
            send_sem=i_send.at[offset], recv_sem=i_recv.at[offset],
            device_id={"wide": inner_peer}, device_id_type=pl.DeviceIdType.MESH,
        )

    @pl.loop(1, outer_n)
    def _(offset):
        along(offset, kv_all.at[wide], wide).start()

    across(0, wide).start()

    @pl.loop(1, outer_n)
    def _(offset):
        slot = outer_at(outer_n - offset)
        along(offset, kv_all.at[slot], slot).wait_recv()
        across(offset, slot).start()

    @pl.loop(0, outer_n)
    def _(offset):
        slot = outer_at(outer_n - offset)
        across(offset, slot + 1 - 2 * inner).wait_recv()
        across(offset, slot).wait_send()

    @pl.loop(1, outer_n)
    def _(offset):
        along(offset, kv_all.at[wide], wide).wait_send()

    for copy in sent:
        copy.wait_send()


def attention_kernel(length, queries, own_kv, cosine, sine, kv_all, kv_mine, out, kv_cache):
    question = pl.program_id(1)
    tokens = queries.shape[1]
    groups = queries.shape[2] // HD
    keys_n = kv_all.shape[0] * kv_all.shape[2]
    kv_cache[...] = kv_mine[...]
    cos, sin = cosine[0], sine[0]
    factor = HD ** (-0.5) * 1.4426950408889634
    cos_q, sin_q = cos * factor, sin * factor

    def rotate(rows, c, s):
        rows = rows.astype(F32)
        return (rows * c + pltpu.roll(rows, HD // 2, 1) * s).astype(BF16)

    own_key = rotate(own_kv[0, 0], cos, sin)
    own_value = own_kv[1, 0]
    pair = 2
    rows_n = tokens * pair
    causal = iota((rows_n, tokens), 0) % tokens >= iota((rows_n, tokens), 1)
    live = iota((rows_n, HD), 0) % tokens < length[question]
    for g in range(0, groups, pair):
        query = jnp.concatenate(
            [
                rotate(queries[0, :, HD * k : HD * (k + 1)], cos_q, sin_q)
                for k in range(g, g + pair)
            ],
            axis=0,
        )
        own = jnp.where(causal, dot_t(query, own_key), -1e30)
        scores = dot_t(query, kv_all[:, 0].reshape(keys_n, HD))
        top = jnp.maximum(
            jnp.max(scores, axis=1, keepdims=True), jnp.max(own, axis=1, keepdims=True)
        )
        weights = jnp.exp2(scores - top)
        own_w = jnp.exp2(own - top)
        denom = jnp.sum(weights, axis=1, keepdims=True) + jnp.sum(own_w, axis=1, keepdims=True)
        mixed = dot(weights.astype(BF16), kv_all[:, 1].reshape(keys_n, HD))
        mixed += dot(own_w.astype(BF16), own_value)
        mixed = jnp.where(live, mixed * (1.0 / denom), 0.0).astype(BF16)
        for k in range(pair):
            out[0, :, HD * (g + k) : HD * (g + k + 1)] = mixed[tokens * k : tokens * (k + 1)]


def both_halves(head_dim):
    freqs = np.power(1000000.0, -np.arange(head_dim // 2) * 2.0 / head_dim).astype(np.float32)
    return np.concatenate([freqs, freqs])


def turns(angles):
    half = angles.shape[-1] // 2
    sign = np.repeat(np.array([-1.0, 1.0], np.float32), half)
    return jnp.cos(angles), jnp.sin(angles) * sign


def mrope_angles(positions, head_dim):
    first_cut = head_dim // 8
    second_cut = first_cut + 3 * head_dim // 16
    place = positions.astype(F32)[:, :, None]
    lane = (np.arange(head_dim) % (head_dim // 2))[None, :]
    chosen = jnp.where(lane < first_cut, place[0], jnp.where(lane < second_cut, place[1], place[2]))
    return chosen * both_halves(head_dim)


def per_device(
    n_wide,
    patches,
    window_ids,
    vit_gain,
    vit_qkv,
    vit_qkv_bias,
    vit_proj,
    vit_proj_bias,
    merge_gain,
    merge_up,
    merge_up_bias,
    merge_down,
    merge_down_bias,
    input_gain,
    kv_weight,
    kv_bias,
    key_positions,
    queries,
    question_kv,
    question_start,
    question_length,
):
    rows_n, part_w = patches.shape
    patches = patches.T
    width = vit_proj.shape[1]
    block = rows_n // 4
    merged_block = block // 4
    d_wide = merge_down.shape[1]
    chunk = d_wide // CHUNKS
    hidden_n = merge_up.shape[1]
    kv_w = kv_weight.shape[2]
    key_cos, key_sin = turns(mrope_angles(key_positions, HD))
    tokens = queries.shape[1]
    place = (question_start[:, None] + jnp.arange(tokens, dtype=jnp.int32)[None, :]).astype(F32)
    query_cos, query_sin = turns(place[:, :, None] * both_halves(HD))

    vmem = pl.BlockSpec(memory_space=pltpu.VMEM)
    hbm = pl.BlockSpec(memory_space=pl.ANY)
    copies = 12 + 5 * CHUNKS
    kv_mine, kv_all = pl.pallas_call(
        functools.partial(vision_kernel, n_wide),
        out_shape=(
            jax.ShapeDtypeStruct((2, block, kv_w), BF16),
            jax.ShapeDtypeStruct((n_wide, 2, block, kv_w), BF16),
        ),
        in_specs=[vmem] * 12 + [hbm] * 5,
        out_specs=(vmem, vmem),
        scratch_shapes=[
            pltpu.VMEM((3, part_w, width), BF16),
            pltpu.VMEM(vit_proj.shape, BF16),
            pltpu.VMEM(merge_up.shape, BF16),
            pltpu.VMEM(merge_down.shape, BF16),
            pltpu.VMEM(kv_weight.shape, BF16),
            pltpu.SemaphoreType.DMA((5,)),
            pltpu.VMEM((4, part_w, rows_n), BF16),
            pltpu.VMEM((width, rows_n), BF16),
            pltpu.VMEM((part_w, rows_n), BF16),
            pltpu.VMEM((rows_n, width), F32),
            pltpu.VMEM((2, block, width), BF16),
            pltpu.VMEM((2, block, width), BF16),
            pltpu.VMEM((block, width), BF16),
            pltpu.VMEM((block, width), BF16),
            pltpu.VMEM((4, merged_block, 4 * width), BF16),
            pltpu.VMEM((block, hidden_n), F32),
            pltpu.VMEM((block, hidden_n), BF16),
            pltpu.VMEM((CHUNKS, block, chunk), F32),
            pltpu.VMEM((CHUNKS, 2, merged_block, chunk), BF16),
            pltpu.VMEM((CHUNKS, 2, merged_block, chunk), BF16),
            pltpu.VMEM((CHUNKS, merged_block, chunk), BF16),
            pltpu.VMEM((CHUNKS, merged_block, chunk), BF16),
            pltpu.VMEM((CHUNKS, 4, merged_block, chunk), BF16),
            pltpu.VMEM((4, merged_block, HD), F32),
            pltpu.VMEM((2, block, kv_w), F32),
            pltpu.SemaphoreType.DMA((copies,)),
            pltpu.SemaphoreType.DMA((copies,)),
            pltpu.SemaphoreType.DMA((n_wide // 2 - 1,)),
            pltpu.SemaphoreType.DMA((n_wide // 2 - 1,)),
            pltpu.SemaphoreType.DMA((n_wide // 2,)),
            pltpu.SemaphoreType.DMA((n_wide // 2,)),
        ],
        compiler_params=pltpu.CompilerParams(
            collective_id=0, has_side_effects=True, vmem_limit_bytes=VMEM_LIMIT
        ),
        name="vision_to_kv",
    )(
        window_ids,
        patches,
        vit_gain,
        vit_qkv_bias,
        vit_proj_bias,
        merge_gain,
        merge_up_bias,
        merge_down_bias.reshape(1, d_wide),
        input_gain.reshape(1, d_wide),
        kv_bias,
        key_cos,
        key_sin,
        vit_qkv.transpose(0, 2, 1),
        vit_proj,
        merge_up,
        merge_down,
        kv_weight,
    )
    q_count = queries.shape[0]
    kv_heads = kv_w // HD
    group_w = queries.shape[2] // kv_heads
    return pl.pallas_call(
        attention_kernel,
        grid_spec=pltpu.PrefetchScalarGridSpec(
            num_scalar_prefetch=1,
            grid=(kv_heads, q_count),
            in_specs=[
                pl.BlockSpec((1, tokens, group_w), lambda h, q, n: (q, 0, h)),
                pl.BlockSpec((2, 1, tokens, HD), lambda h, q, n: (0, q, 0, h)),
                pl.BlockSpec((1, tokens, HD), lambda h, q, n: (q, 0, 0)),
                pl.BlockSpec((1, tokens, HD), lambda h, q, n: (q, 0, 0)),
                pl.BlockSpec((n_wide, 2, block, HD), lambda h, q, n: (0, 0, 0, h)),
                pl.BlockSpec((2, block, HD), lambda h, q, n: (0, 0, h)),
            ],
            out_specs=(
                pl.BlockSpec((1, tokens, group_w), lambda h, q, n: (q, 0, h)),
                pl.BlockSpec((2, block, HD), lambda h, q, n: (0, 0, h)),
            ),
        ),
        out_shape=(
            jax.ShapeDtypeStruct(queries.shape, BF16),
            jax.ShapeDtypeStruct((2, block, kv_w), BF16),
        ),
        compiler_params=pltpu.CompilerParams(vmem_limit_bytes=VMEM_LIMIT),
        name="question_attention",
    )(question_length, queries, question_kv, query_cos, query_sin, kv_all, kv_mine)


def solution(mesh):
    return jax.shard_map(
        functools.partial(per_device, mesh.shape["wide"]),
        mesh=mesh,
        in_specs=(
            P("wide", "narrow"),
            P("wide", None),
            P(),
            P(None, None, "narrow"),
            P(None, "narrow"),
            P("narrow", None),
            P(),
            P(),
            P(None, "narrow"),
            P("narrow"),
            P("narrow", None),
            P(),
            P(),
            P(None, None, "narrow"),
            P(None, "narrow"),
            P(None, "wide"),
            P("wide", None, "narrow"),
            P(None, "wide", None, "narrow"),
            P("wide"),
            P("wide"),
        ),
        out_specs=(P("wide", None, "narrow"), P(None, "wide", "narrow")),
        check_vma=False,
    )
```

```python
import functools
import math

import jax
import jax.numpy as jnp
import numpy as np
from jax import lax
from jax.experimental import pallas as pl
from jax.experimental.pallas import tpu as pltpu
from jax.sharding import PartitionSpec as P

HD = 128
VHD = 80
CHUNKS = 8
PAIR = 4
LAGS = (2, 5, 8, 10)
F32 = jnp.float32
BF16 = jnp.bfloat16
PI_PARTS = (3.140625, 0.0009675025939941406, 1.5099580252808664e-07)
VMEM_LIMIT = 60 * 1024 * 1024


def dot(a, b):
    return jnp.dot(a, b, preferred_element_type=F32)


def dot_t(a, b):
    return lax.dot_general(a, b, (((1,), (1,)), ((), ())), preferred_element_type=F32)


def iota(shape, axis):
    return lax.broadcasted_iota(jnp.int32, shape, axis)


def dot_0(a, b):
    return lax.dot_general(a, b, (((0,), (0,)), ((), ())), preferred_element_type=F32)


def row(ref):
    return ref[...].reshape(1, ref.shape[0])


def column(values):
    n = values.shape[1]
    return jnp.sum(
        jnp.where(iota((n, n), 0) == iota((n, n), 1), values, 0.0), axis=1, keepdims=True
    )


def turns(angles):
    turn = jnp.floor(angles * np.float32(1.0 / np.pi) + 0.5)
    rest = ((angles - turn * PI_PARTS[0]) - turn * PI_PARTS[1]) - turn * PI_PARTS[2]
    odd = turn - 2.0 * jnp.floor(turn * 0.5)
    flip = 1.0 - 2.0 * odd
    square = rest * rest
    sine = rest
    cosine = jnp.ones_like(rest)
    s_sum, c_sum = jnp.zeros_like(rest), jnp.zeros_like(rest)
    for k in range(7, 0, -1):
        s_sum = (s_sum + (-1.0) ** k / math.factorial(2 * k + 1)) * square
        c_sum = (c_sum + (-1.0) ** k / math.factorial(2 * k)) * square
    sine = (sine + sine * s_sum) * flip
    cosine = (cosine + c_sum) * flip
    return cosine, jnp.where(iota(angles.shape, 1) < angles.shape[1] // 2, -sine, sine)


def vision_kernel(
    n_wide,
    ids, patches, gain, qkv_bias, proj_bias, merge_gain, up_bias, down_bias, input_gain,
    kv_bias, positions, freqs,
    qkv_hbm, proj_hbm, up_hbm, down_hbm, kvw_hbm,
    kv_out, kv_all,
    qkv_w, proj_w, up_w, down_w, kv_w, w_sem,
    rows, normed, heads, partial, give, got, x_give, x_got, merged, up_acc, up_act,
    d_part, d_give, d_got, dx_give, dx_got, emb, squares, kv_acc, key_cos, key_sin,
    send_sem, recv_sem, o_send, o_recv, i_send, i_recv,
):
    me = lax.axis_index("narrow")
    x, core = me // 2, me % 2
    cp = x * 2 + (1 - core)
    xp = (1 - x) * 2 + core
    dg = (1 - x) * 2 + (1 - core)
    part_w, row_count = patches.shape
    width = proj_hbm.shape[1]
    block = row_count // 4
    merged_block = block // 4
    wide_d = down_hbm.shape[1]
    chunk = wide_d // CHUNKS
    wide = lax.axis_index("wide")
    outer_n = n_wide // 2
    outer, inner = wide // 2, wide % 2
    inner_peer = outer * 2 + (1 - inner)

    def outer_at(offset):
        return ((outer + offset) % outer_n) * 2 + inner

    def local(index, src, dst):
        return pltpu.make_async_copy(src, dst, w_sem.at[index])

    def remote(index, src, dst, peer):
        return pltpu.make_async_remote_copy(
            src_ref=src, dst_ref=dst, send_sem=send_sem.at[index], recv_sem=recv_sem.at[index],
            device_id={"narrow": peer}, device_id_type=pl.DeviceIdType.MESH,
        )

    loads = [
        local(0, qkv_hbm, qkv_w), local(1, proj_hbm, proj_w), local(2, up_hbm, up_w),
        local(3, down_hbm, down_w), local(4, kvw_hbm, kv_w),
    ]
    loads[0].start()
    loads[1].start()

    barrier = pltpu.get_barrier_semaphore()

    def greet(peer):
        pl.semaphore_signal(barrier, inc=1, device_id=peer, device_id_type=pl.DeviceIdType.MESH)

    greet({"narrow": cp})
    greet({"narrow": xp})
    greet({"wide": inner_peer})

    @pl.loop(1, outer_n)
    def _(offset):
        greet({"wide": outer_at(offset)})

    pl.semaphore_wait(barrier, outer_n + 2)

    sent = []

    def send(index, src, dst, peer):
        copy = remote(index, src, dst, peer)
        copy.start()
        sent.append(copy)

    def arrived(index, dst, peer):
        remote(index, dst, dst, peer).wait_recv()

    def gather_start(index, src, slots):
        send(index + 1, src, slots.at[me], xp)
        send(index, src, slots.at[me], cp)

    def gather_forward(index, slots):
        arrived(index + 1, slots.at[xp], xp)
        send(index + 2, slots.at[xp], slots.at[xp], cp)

    def gather_finish(index, slots):
        arrived(index, slots.at[cp], cp)
        arrived(index + 2, slots.at[dg], cp)

    gather_start(0, patches, rows)
    loads[2].start()
    rows[me] = patches[...]
    ids_row = ids[...].astype(F32)
    token_of = (iota((row_count, row_count // 4), 0) // 4 == iota((row_count, row_count // 4), 1))
    token_of = token_of.astype(F32)
    patch_col = jnp.sum(token_of * ids_row, axis=1, keepdims=True)
    patch_row = dot_t(
        jnp.broadcast_to(ids_row, (8, row_count // 4)).astype(BF16), token_of.astype(BF16)
    )[:1]
    same = patch_col == patch_row
    lane = iota((1, HD), 1) % (HD // 2)
    places = [column(positions[k : k + 1, :].astype(F32)) for k in range(3)]
    chosen = jnp.where(
        lane < HD // 8, places[0], jnp.where(lane < HD // 8 + 3 * HD // 16, places[1], places[2])
    )
    key_cos[...], key_sin[...] = turns(chosen * freqs[...])
    gather_forward(0, rows)
    gather_finish(0, rows)
    loads[3].start()
    loads[4].start()

    total_sq = jnp.zeros((1, row_count), F32)
    for i in range(4):
        part = rows[i].astype(F32)
        total_sq += jnp.sum(part * part, axis=0, keepdims=True)
    scale = lax.rsqrt(total_sq / width + 1e-06)
    features = rows[...].reshape(width, row_count)
    gains = row(gain)
    for i in range(0, width, 128):
        normed[i : i + 128, :] = (
            features[i : i + 128].astype(F32) * scale * column(gains[:, i : i + 128])
        ).astype(BF16)
    loads[0].wait()
    query, key, value = [
        (dot(qkv_w[which], normed[...]) + column(qkv_bias[which : which + 1, :])).astype(BF16)
        for which in range(3)
    ]
    for h in range(part_w // VHD):
        at = slice(VHD * h, VHD * (h + 1))
        scores = dot_0(key[at], query[at]) * VHD ** (-0.5)
        weights = jnp.where(same, jnp.exp(scores), 0.0)
        denom = 1.0 / jnp.sum(weights, axis=0, keepdims=True)
        heads[at, :] = (dot(value[at], weights.astype(BF16)) * denom).astype(BF16)
    loads[1].wait()
    partial[...] = dot_0(heads[...], proj_w[...])

    def rows_of(ref, index, size):
        return ref[pl.ds(pl.multiple_of(index * size, size), size), :]

    give[0] = rows_of(partial, dg, block).astype(BF16)
    send(3, give.at[0], got.at[0], cp)
    give[1] = rows_of(partial, cp, block).astype(BF16)
    send(4, give.at[1], got.at[1], cp)
    mine = iota((block, row_count), 1) - block * me == iota((block, row_count), 0)
    resid = dot_t(mine.astype(F32).astype(BF16), features) + row(proj_bias)
    arrived(3, got.at[0], cp)
    x_give[...] = (rows_of(partial, xp, block) + got[0].astype(F32)).astype(BF16)
    send(5, x_give, x_got, xp)
    arrived(4, got.at[1], cp)
    hidden = resid + rows_of(partial, me, block) + got[1].astype(F32)
    arrived(5, x_got, xp)
    hidden = hidden + x_got[...].astype(F32)
    hidden_sq = jnp.sum(hidden * hidden, axis=1, keepdims=True) / width
    hidden_n = (hidden * lax.rsqrt(hidden_sq + 1e-06) * row(merge_gain)).astype(BF16)
    to_row = iota((block, block), 0)
    order = (to_row % merged_block) * 4 + to_row // merged_block == iota((block, block), 1)
    ordered = dot(order.astype(F32).astype(BF16), hidden_n).astype(BF16)
    for j in range(4):
        merged[me, :, width * j : width * (j + 1)] = ordered[
            merged_block * j : merged_block * (j + 1)
        ]
    gather_start(6, merged.at[me], merged)
    gather_forward(6, merged)
    gather_finish(6, merged)

    loads[2].wait()
    up_acc[...] = jnp.zeros_like(up_acc)
    step = 512

    @pl.loop(0, up_hbm.shape[0] // step)
    def _(kk):
        at = pl.ds(pl.multiple_of(kk * step, step), step)
        up_acc[...] += dot(merged[:, :, at].reshape(block, step), up_w[at, :])

    pre = up_acc[...] + row(up_bias)
    up_act[...] = (0.5 * pre * (1.0 + lax.erf(pre * 0.7071067811865476))).astype(BF16)
    loads[3].wait()
    kv_acc[...] = jnp.zeros_like(kv_acc)
    square_sum = jnp.zeros((merged_block, 1), F32)
    for t in range(CHUNKS + LAGS[3]):
        c = t
        if c < CHUNKS:
            d_part[c] = dot(up_act[...], down_w[:, chunk * c : chunk * (c + 1)])
            d_give[c, 0] = rows_of(d_part.at[c], dg, merged_block).astype(BF16)
            d_give[c, 1] = rows_of(d_part.at[c], cp, merged_block).astype(BF16)
            send(12 + 5 * c, d_give.at[c], d_got.at[c], cp)
        c = t - LAGS[0]
        if 0 <= c < CHUNKS:
            arrived(12 + 5 * c, d_got.at[c], cp)
            dx_give[c] = (
                rows_of(d_part.at[c], xp, merged_block) + d_got[c, 0].astype(F32)
            ).astype(BF16)
            send(13 + 5 * c, dx_give.at[c], dx_got.at[c], xp)
        c = t - LAGS[1]
        if 0 <= c < CHUNKS:
            arrived(13 + 5 * c, dx_got.at[c], xp)
            cols = slice(chunk * c, chunk * (c + 1))
            embed = rows_of(d_part.at[c], me, merged_block) + d_got[c, 1].astype(F32)
            embed = embed + dx_got[c].astype(F32) + down_bias[:, cols]
            square_sum += jnp.sum(embed * embed, axis=1, keepdims=True)
            emb[c, me] = (embed * input_gain[:, cols]).astype(BF16)
            gather_start(14 + 5 * c, emb.at[c, me], emb.at[c])
            if c == CHUNKS - 1:
                squares[me] = jnp.broadcast_to(square_sum, squares.shape[1:])
                gather_start(9, squares.at[me], squares)
        c = t - LAGS[2]
        if 0 <= c < CHUNKS:
            gather_forward(14 + 5 * c, emb.at[c])
            if c == CHUNKS - 1:
                gather_forward(9, squares)
        c = t - LAGS[3]
        if 0 <= c < CHUNKS:
            gather_finish(14 + 5 * c, emb.at[c])
            if c == 0:
                loads[4].wait()
            lhs = emb[c].reshape(block, chunk)
            for which in range(2):
                kv_acc[which] += dot(lhs, kv_w[which, chunk * c : chunk * (c + 1), :])
    gather_finish(9, squares)
    row_scale = lax.rsqrt(squares[...].reshape(block, squares.shape[2]) / wide_d + 1e-06)
    for h in range(kv_w.shape[2] // HD):
        cols = slice(HD * h, HD * (h + 1))
        raw = kv_acc[0, :, cols] * row_scale + kv_bias[0:1, cols]
        rotated = raw * key_cos[...] + pltpu.roll(raw, HD // 2, 1) * key_sin[...]
        kv_out[0, :, cols] = rotated.astype(BF16)
        kv_out[1, :, cols] = (kv_acc[1, :, cols] * row_scale + kv_bias[1:2, cols]).astype(BF16)
    kv_all[wide] = kv_out[...]

    def along(offset, src, slot):
        return pltpu.make_async_remote_copy(
            src_ref=src, dst_ref=kv_all.at[slot],
            send_sem=o_send.at[offset - 1], recv_sem=o_recv.at[offset - 1],
            device_id={"wide": outer_at(offset)}, device_id_type=pl.DeviceIdType.MESH,
        )

    def across(offset, slot):
        return pltpu.make_async_remote_copy(
            src_ref=kv_all.at[slot], dst_ref=kv_all.at[slot],
            send_sem=i_send.at[offset], recv_sem=i_recv.at[offset],
            device_id={"wide": inner_peer}, device_id_type=pl.DeviceIdType.MESH,
        )

    @pl.loop(1, outer_n)
    def _(offset):
        along(offset, kv_all.at[wide], wide).start()

    across(0, wide).start()

    @pl.loop(1, outer_n)
    def _(offset):
        slot = outer_at(outer_n - offset)
        along(offset, kv_all.at[slot], slot).wait_recv()
        across(offset, slot).start()

    @pl.loop(0, outer_n)
    def _(offset):
        slot = outer_at(outer_n - offset)
        across(offset, slot + 1 - 2 * inner).wait_recv()
        across(offset, slot).wait_send()

    @pl.loop(1, outer_n)
    def _(offset):
        along(offset, kv_all.at[wide], wide).wait_send()

    for copy in sent:
        copy.wait_send()


def attention_kernel(
    length, start, queries, own_kv, freqs, kv_all, kv_mine, out, kv_cache, keys_t, values
):
    question = pl.program_id(1)
    tokens = queries.shape[1]
    groups = queries.shape[2] // HD
    keys_n = kv_all.shape[0] * kv_all.shape[2]

    @pl.when(question == 0)
    def _():
        kv_cache[...] = kv_mine[...]
        keys_t[...] = kv_all[:, 0].reshape(keys_n, HD).astype(F32).T.astype(BF16)
        values[:, :HD] = kv_all[:, 1].reshape(keys_n, HD)
        values[:, HD:] = jnp.ones((keys_n, HD), BF16)

    place = (start[question] + iota((tokens, HD), 0)).astype(F32)
    cos, sin = turns(place * freqs[...])
    factor = HD ** (-0.5) * 1.4426950408889634
    cos_q, sin_q = cos * factor, sin * factor

    def rotate(rows, c, s):
        rows = rows.astype(F32)
        return rows * c + pltpu.roll(rows, HD // 2, 1) * s

    own_key = rotate(own_kv[0, 0], cos, sin).T.astype(BF16)
    own_value = jnp.concatenate([own_kv[1, 0], jnp.ones((tokens, HD), BF16)], axis=1)
    rows_n = tokens * PAIR
    causal = iota((rows_n, tokens), 0) % tokens >= iota((rows_n, tokens), 1)
    live = iota((rows_n, HD), 0) % tokens < length[question]
    for g in range(0, groups, PAIR):
        query = jnp.concatenate(
            [
                rotate(queries[0, :, HD * k : HD * (k + 1)], cos_q, sin_q).astype(BF16)
                for k in range(g, g + PAIR)
            ],
            axis=0,
        )
        own = jnp.where(causal, dot(query, own_key), -1e30)
        scores = dot(query, keys_t[...])
        top = jnp.maximum(
            jnp.max(scores, axis=1, keepdims=True), jnp.max(own, axis=1, keepdims=True)
        )
        mixed = dot(jnp.exp2(scores - top).astype(BF16), values[...])
        mixed += dot(jnp.exp2(own - top).astype(BF16), own_value)
        mixed = jnp.where(live, mixed[:, :HD] / mixed[:, HD:], 0.0).astype(BF16)
        for k in range(PAIR):
            out[0, :, HD * (g + k) : HD * (g + k + 1)] = mixed[tokens * k : tokens * (k + 1)]


def both_halves(head_dim):
    freqs = np.power(1000000.0, -np.arange(head_dim // 2) * 2.0 / head_dim).astype(np.float32)
    return np.concatenate([freqs, freqs])


def per_device(
    n_wide,
    patches,
    window_ids,
    vit_gain,
    vit_qkv,
    vit_qkv_bias,
    vit_proj,
    vit_proj_bias,
    merge_gain,
    merge_up,
    merge_up_bias,
    merge_down,
    merge_down_bias,
    input_gain,
    kv_weight,
    kv_bias,
    key_positions,
    queries,
    question_kv,
    question_start,
    question_length,
):
    rows_n, part_w = patches.shape
    patches = patches.T
    width = vit_proj.shape[1]
    block = rows_n // 4
    merged_block = block // 4
    d_wide = merge_down.shape[1]
    chunk = d_wide // CHUNKS
    hidden_n = merge_up.shape[1]
    kv_w = kv_weight.shape[2]
    tokens = queries.shape[1]
    freqs = jnp.asarray(both_halves(HD)[None, :])

    vmem = pl.BlockSpec(memory_space=pltpu.VMEM)
    hbm = pl.BlockSpec(memory_space=pl.ANY)
    copies = 12 + 5 * CHUNKS
    kv_mine, kv_all = pl.pallas_call(
        functools.partial(vision_kernel, n_wide),
        out_shape=(
            jax.ShapeDtypeStruct((2, block, kv_w), BF16),
            jax.ShapeDtypeStruct((n_wide, 2, block, kv_w), BF16),
        ),
        in_specs=[vmem] * 12 + [hbm] * 5,
        out_specs=(vmem, vmem),
        scratch_shapes=[
            pltpu.VMEM((3, part_w, width), BF16),
            pltpu.VMEM(vit_proj.shape, BF16),
            pltpu.VMEM(merge_up.shape, BF16),
            pltpu.VMEM(merge_down.shape, BF16),
            pltpu.VMEM(kv_weight.shape, BF16),
            pltpu.SemaphoreType.DMA((5,)),
            pltpu.VMEM((4, part_w, rows_n), BF16),
            pltpu.VMEM((width, rows_n), BF16),
            pltpu.VMEM((part_w, rows_n), BF16),
            pltpu.VMEM((rows_n, width), F32),
            pltpu.VMEM((2, block, width), BF16),
            pltpu.VMEM((2, block, width), BF16),
            pltpu.VMEM((block, width), BF16),
            pltpu.VMEM((block, width), BF16),
            pltpu.VMEM((4, merged_block, 4 * width), BF16),
            pltpu.VMEM((block, hidden_n), F32),
            pltpu.VMEM((block, hidden_n), BF16),
            pltpu.VMEM((CHUNKS, block, chunk), F32),
            pltpu.VMEM((CHUNKS, 2, merged_block, chunk), BF16),
            pltpu.VMEM((CHUNKS, 2, merged_block, chunk), BF16),
            pltpu.VMEM((CHUNKS, merged_block, chunk), BF16),
            pltpu.VMEM((CHUNKS, merged_block, chunk), BF16),
            pltpu.VMEM((CHUNKS, 4, merged_block, chunk), BF16),
            pltpu.VMEM((4, merged_block, HD), F32),
            pltpu.VMEM((2, block, kv_w), F32),
            pltpu.VMEM((block, HD), F32),
            pltpu.VMEM((block, HD), F32),
            pltpu.SemaphoreType.DMA((copies,)),
            pltpu.SemaphoreType.DMA((copies,)),
            pltpu.SemaphoreType.DMA((n_wide // 2 - 1,)),
            pltpu.SemaphoreType.DMA((n_wide // 2 - 1,)),
            pltpu.SemaphoreType.DMA((n_wide // 2,)),
            pltpu.SemaphoreType.DMA((n_wide // 2,)),
        ],
        compiler_params=pltpu.CompilerParams(
            collective_id=0, has_side_effects=True, vmem_limit_bytes=VMEM_LIMIT
        ),
        name="vision_to_kv",
    )(
        window_ids,
        patches,
        vit_gain,
        vit_qkv_bias,
        vit_proj_bias,
        merge_gain,
        merge_up_bias,
        merge_down_bias.reshape(1, d_wide),
        input_gain.reshape(1, d_wide),
        kv_bias,
        key_positions,
        freqs,
        vit_qkv.transpose(0, 2, 1),
        vit_proj,
        merge_up,
        merge_down,
        kv_weight,
    )
    q_count = queries.shape[0]
    kv_heads = kv_w // HD
    group_w = queries.shape[2] // kv_heads
    return pl.pallas_call(
        attention_kernel,
        grid_spec=pltpu.PrefetchScalarGridSpec(
            num_scalar_prefetch=2,
            grid=(kv_heads, q_count),
            in_specs=[
                pl.BlockSpec((1, tokens, group_w), lambda h, q, n, p: (q, 0, h)),
                pl.BlockSpec((2, 1, tokens, HD), lambda h, q, n, p: (0, q, 0, h)),
                pl.BlockSpec((1, HD), lambda h, q, n, p: (0, 0)),
                pl.BlockSpec((n_wide, 2, block, HD), lambda h, q, n, p: (0, 0, 0, h)),
                pl.BlockSpec((2, block, HD), lambda h, q, n, p: (0, 0, h)),
            ],
            out_specs=(
                pl.BlockSpec((1, tokens, group_w), lambda h, q, n, p: (q, 0, h)),
                pl.BlockSpec((2, block, HD), lambda h, q, n, p: (0, 0, h)),
            ),
            scratch_shapes=[
                pltpu.VMEM((HD, n_wide * block), BF16),
                pltpu.VMEM((n_wide * block, 2 * HD), BF16),
            ],
        ),
        out_shape=(
            jax.ShapeDtypeStruct(queries.shape, BF16),
            jax.ShapeDtypeStruct((2, block, kv_w), BF16),
        ),
        compiler_params=pltpu.CompilerParams(vmem_limit_bytes=VMEM_LIMIT),
        name="question_attention",
    )(question_length, question_start, queries, question_kv, freqs, kv_all, kv_mine)


def solution(mesh):
    return jax.shard_map(
        functools.partial(per_device, mesh.shape["wide"]),
        mesh=mesh,
        in_specs=(
            P("wide", "narrow"),
            P("wide", None),
            P(),
            P(None, None, "narrow"),
            P(None, "narrow"),
            P("narrow", None),
            P(),
            P(),
            P(None, "narrow"),
            P("narrow"),
            P("narrow", None),
            P(),
            P(),
            P(None, None, "narrow"),
            P(None, "narrow"),
            P(None, "wide"),
            P("wide", None, "narrow"),
            P(None, "wide", None, "narrow"),
            P("wide"),
            P("wide"),
        ),
        out_specs=(P("wide", None, "narrow"), P(None, "wide", "narrow")),
        check_vma=False,
    )
```
